32 devices in a mesh: wide: 16 (over z, x, core), narrow: 2 (over y).
Axes of the slice: x: 2, y: 2, z: 4, core: 2. Of those that a mesh axis runs over, the one named last changes fastest.
Arguments:
- frames: bfloat16 [32, 448, 768], P(('wide', 'narrow')), may hold values from -6 to 6
- dec_in: bfloat16 [32, 448, 768], P(('wide', 'narrow')), may hold values from -6 to 6
- cotangent: bfloat16 [32, 448, 768], P(('wide', 'narrow')), may hold values from -6 to 6
- dec_len: int32 [32], replicated, may hold values from 1 to 448, as said below
- bucket: int32 [32], replicated, may hold values from 0 to 3
- enc_weights: bfloat16 [9216, 768], P(('wide', 'narrow')), may hold values from -0.3247595 to 0.3247595
- enc_vectors: bfloat16 [9216], P(('wide', 'narrow')), may hold values from -0.75 to 1.46, as said below
- dec_weights: bfloat16 [12288, 768], P(('wide', 'narrow')), may hold values from -0.3247595 to 0.3247595
- dec_vectors: bfloat16 [13056], P(('wide', 'narrow')), may hold values from -0.75 to 1.46, as said below
Outputs:
- dec_out: bfloat16 [32, 448, 768], P(('wide', 'narrow'))
- d_dec_in: float32 [32, 448, 768], P(('wide', 'narrow'))
- d_enc: float32 [32, 448, 768], P(('wide', 'narrow'))
- d_dec_weights: float32 [12288, 768], P(('wide', 'narrow'))
- d_dec_vectors: float32 [13056], P(('wide', 'narrow'))
The draws below stay inside these ranges and needn't reach their ends.
Inputs may be any that keep to these rules, and one draw needn't show every extreme that they name: `dec_len`: some item has exactly 448 tokens; most have few. `enc_vectors`: gains lie in 0.55 to 1.46, biases in -0.75 to 0.75. `dec_vectors`: gains lie in 0.55 to 1.46, biases in -0.75 to 0.75.
All inputs are finite; a program needn't handle non-finite values.
Results may differ from the reference program's by a relative error of at most 0.025.
Values may be sent and summed in bfloat16 or wider, within the bound.
No kernel may reach another device: no remote copies, remote signals or barrier semaphores. Data moves between devices by JAX's collectives and lax.ppermute only.
A program may use at most 192 MiB of HBM per device.

```python
import math
import jax
import jax.numpy as jnp
from jax import lax

D = 768
HEADS = 12
FF = 3072
FRAMES = 448
L_DEC = 448
NBUCKET = 4
BATCH = 32
N_NARROW = 2


def scaled_stack(key, number):
    rows = number * D + 2 * FF
    raw = jnp.clip(jax.random.normal(key, (rows, D), jnp.float32), -3.0, 3.0)
    index = jnp.arange(rows)[:, None]
    block = index // D
    attn_scale = jnp.where(block % 4 == 3, 3.0, 1.0) * D ** (-0.5)
    scale = jnp.where(index < number * D, attn_scale, jnp.where(index < number * D + FF, D ** (-0.5), 1.5 * FF ** (-0.5)))
    return raw * scale


def scaled_vector(key, number, gain_end):
    total = number * D + FF
    raw = jnp.clip(jax.random.normal(key, (total,), jnp.float32), -3.0, 3.0)
    index = jnp.arange(total)
    is_gain = (index < gain_end * D) & (index // D % 2 == 0)
    return jnp.where(is_gain, 1.0 + 0.15 * raw, 0.25 * raw)


def draw_enc_weights(key, part):
    return scaled_stack(jax.random.fold_in(key, 11), 4).astype(jnp.bfloat16)


def draw_dec_weights(key, part):
    return scaled_stack(jax.random.fold_in(key, 12), 8).astype(jnp.bfloat16)


def draw_enc_vectors(key, part):
    return scaled_vector(jax.random.fold_in(key, 13), 8, 4).astype(jnp.bfloat16)


def draw_dec_vectors(key, part):
    return scaled_vector(jax.random.fold_in(key, 14), 13, 6).astype(jnp.bfloat16)


def draw_dec_len(key, part):
    first, second, third, fourth = jax.random.split(jax.random.fold_in(key, 15), 4)
    factor_one = jax.random.randint(first, (BATCH,), 1, L_DEC + 1)
    factor_two = jax.random.randint(second, (BATCH,), 1, L_DEC + 1)
    factor_three = jax.random.randint(third, (BATCH,), 1, L_DEC + 1)
    lengths = jnp.maximum(1, factor_one * factor_two * factor_three // (L_DEC * L_DEC))
    longest = jax.random.randint(fourth, (), 0, BATCH)
    lengths = jnp.where(jnp.arange(BATCH) == longest, L_DEC, lengths)
    return lengths.astype(jnp.int32)


def place_ends(array, rng, low, top_value):
    extent = array.shape
    place = [jax.random.randint(jax.random.fold_in(rng, axis), (), 0, extent[axis]) for axis in range(len(extent))]
    array = array.at[tuple(place)].set(low)
    longest = extent.index(max(extent))
    place[longest] = (place[longest] + 1) % extent[longest]
    return array.at[tuple(place)].set(top_value)


def shard_levels(stream_key, dims, cuts, smallest, high):
    factor_of = 1.0
    for axis_at, blocks in cuts:
        steps = jax.random.uniform(jax.random.fold_in(jax.random.fold_in(stream_key, 6), axis_at), (blocks,), jnp.float32, smallest / len(cuts), high / len(cuts))
        factor_of = factor_of * jnp.repeat(jnp.exp(steps), dims[axis_at] // blocks).reshape((-1,) + (1,) * (len(dims) - 1 - axis_at))
    return factor_of


def gaussian(stream_key, extent, scale, reach, cuts=(), held_as=jnp.bfloat16):
    drawn = scale * jax.random.normal(stream_key, extent, jnp.float32)
    if cuts:
        drawn = drawn * shard_levels(stream_key, extent, cuts, -0.22, 0.18)
    return jnp.clip(drawn, -reach, reach).astype(held_as)


def setup_inputs(seed: int = 0) -> dict:
    arg_keys = jax.random.split(jax.random.key(seed), 10)
    return {
        "frames": gaussian(arg_keys[0], (BATCH, FRAMES, D), 1.0, 6.0, ((0, 32),)),
        "dec_in": gaussian(arg_keys[1], (BATCH, L_DEC, D), 1.0, 6.0, ((0, 32),)),
        "cotangent": gaussian(arg_keys[2], (BATCH, L_DEC, D), 1.0, 6.0, ((0, 32),)),
        "dec_len": draw_dec_len(jax.random.fold_in(arg_keys[9], 71), 0),
        "bucket": place_ends(jax.random.randint(arg_keys[4], (BATCH,), 0, NBUCKET), jax.random.fold_in(arg_keys[4], 1), 0, NBUCKET - 1).astype(jnp.int32),
        "enc_weights": draw_enc_weights(jax.random.fold_in(arg_keys[9], 71), 0),
        "enc_vectors": draw_enc_vectors(jax.random.fold_in(arg_keys[9], 71), 0),
        "dec_weights": draw_dec_weights(jax.random.fold_in(arg_keys[9], 71), 0),
        "dec_vectors": draw_dec_vectors(jax.random.fold_in(arg_keys[9], 71), 0),
    }


@jax.custom_vjp
def low(v):
    return lax.optimization_barrier(v.astype(jnp.bfloat16)).astype(jnp.float32)

@jax.custom_vjp
def low_back(v):
    return v

def low_keep(v):
    return (low(v), None)

def low_pass(kept, grad):
    return (grad,)

def back_keep(v):
    return (v, None)

def back_low(kept, grad):
    return (low(grad),)
low.defvjp(low_keep, low_pass)
low_back.defvjp(back_keep, back_low)
EPS = 1e-05
HIGHEST = lax.Precision.HIGHEST

def layer_norm(values, gain, bias):
    mean = lax.optimization_barrier(jnp.mean(values, axis=-1, keepdims=True))
    centred = values - mean
    spread = lax.optimization_barrier(jnp.mean(centred * centred, axis=-1, keepdims=True))
    return centred * lax.rsqrt(spread + EPS) * gain + bias

def product(left, right):
    return jnp.dot(left, right, precision=HIGHEST, preferred_element_type=jnp.float32)

def product_t(left, right):
    return lax.dot_general(left, right, (((1,), (1,)), ((), ())), precision=HIGHEST, preferred_element_type=jnp.float32)

def rounded_both(values):
    return low(low_back(values))

def split_rows(stack, number):
    blocks = [stack[index * D:(index + 1) * D] for index in range(number)]
    return (blocks, stack[number * D:number * D + FF], stack[number * D + FF:])

def split_vector(vector, number):
    parts = [vector[index * D:(index + 1) * D] for index in range(number)]
    return (parts, vector[number * D:])

def by_heads(values):
    return values.reshape(values.shape[0], HEADS, D // HEADS)

def attend(query, keys, values, causal):
    scale = 1.0 / math.sqrt(D // HEADS)
    scores = low_back(jnp.einsum('qhd,khd->hqk', by_heads(query), by_heads(keys), precision=HIGHEST) * scale)
    if causal:
        keep = jnp.arange(query.shape[0])[:, None] >= jnp.arange(keys.shape[0])[None, :]
        scores = jnp.where(keep[None], scores, -1e+30)
    highest = lax.optimization_barrier(jnp.max(scores, axis=-1, keepdims=True))
    weights = jnp.exp(scores - highest)
    probs = low(weights / lax.optimization_barrier(jnp.sum(weights, axis=-1, keepdims=True)))
    mixed = jnp.einsum('hqk,khd->qhd', probs, by_heads(values), precision=HIGHEST)
    return mixed.reshape(query.shape[0], D)

def encode(frame, stack, vector):
    (w_query, w_keys, w_values, w_output), up_weight, down_weight = split_rows(stack, 4)
    (gain_one, bias_one, gain_two, bias_two, bias_query, bias_values, bias_output, bias_down), bias_up = split_vector(vector, 8)
    normed = low(layer_norm(frame, gain_one, bias_one))
    query = low(product(normed, w_query) + bias_query)
    keys = low(product(normed, w_keys))
    values = low(product(normed, w_values) + bias_values)
    mixed = low(attend(query, keys, values, False))
    after_attn = frame + product(mixed, w_output) + bias_output
    normed_two = low(layer_norm(after_attn, gain_two, bias_two))
    hidden = low(jax.nn.gelu(product_t(normed_two, up_weight) + bias_up, approximate=False))
    return low(after_attn + product(hidden, down_weight) + bias_down)

def decode(inputs, memory, length, stack, vector):
    (self_q, self_k, self_v, self_o, cross_q, cross_k, cross_v, cross_o), up_weight, down_weight = split_rows(stack, 8)
    (gain_one, bias_one, gain_two, bias_two, gain_three, bias_three, bias_sq, bias_sv, bias_so, bias_cq, bias_cv, bias_co, bias_down), bias_up = split_vector(vector, 13)
    live = (jnp.arange(L_DEC) < length)[:, None].astype(jnp.float32)
    normed_one = low(layer_norm(inputs, gain_one, bias_one))
    query_self = rounded_both(product(normed_one, self_q) + bias_sq)
    keys_self = rounded_both(product(normed_one, self_k))
    values_self = rounded_both(product(normed_one, self_v) + bias_sv)
    mixed_self = rounded_both(attend(query_self, keys_self, values_self, True))
    after_self = inputs + low_back(product(mixed_self, self_o) + bias_so)
    normed_two = low(layer_norm(after_self, gain_two, bias_two))
    query_cross = rounded_both(product(normed_two, cross_q) + bias_cq)
    keys_cross = rounded_both(product(memory, cross_k))
    values_cross = rounded_both(product(memory, cross_v) + bias_cv)
    mixed_cross = rounded_both(attend(query_cross, keys_cross, values_cross, False))
    after_cross = after_self + low_back(product(mixed_cross, cross_o) + bias_co)
    normed_three = low(layer_norm(after_cross, gain_three, bias_three))
    hidden_pre = low_back(product_t(normed_three, up_weight) + bias_up)
    hidden = low(jax.nn.gelu(hidden_pre, approximate=False))
    result = after_cross + low_back(product(hidden, down_weight) + bias_down)
    return live * result

def arrange_slots(bucket_table):
    members = bucket_table.shape[-1]
    places = jnp.arange(members, dtype=jnp.int32)
    earlier = (bucket_table[:, None, :] < bucket_table[:, :, None]) | (bucket_table[:, None, :] == bucket_table[:, :, None]) & (places[None, None, :] < places[None, :, None])
    return lax.optimization_barrier(jnp.sum(earlier.astype(jnp.int32), axis=2))

def reference(frames, dec_in, cotangent, dec_len, bucket, enc_weights, enc_vectors, dec_weights, dec_vectors):
    enc_stack = enc_weights.astype(jnp.float32)
    enc_vector = enc_vectors.astype(jnp.float32)
    dec_stack = dec_weights.astype(jnp.float32)
    dec_vector = dec_vectors.astype(jnp.float32)
    encoded = lax.map(lambda frame: encode(frame.astype(jnp.float32), enc_stack, enc_vector), frames)
    members = N_NARROW
    rank_table = arrange_slots(bucket.reshape(-1, members))
    base = (jnp.arange(rank_table.shape[0], dtype=jnp.int32) * members)[:, None]
    places = jnp.arange(members, dtype=jnp.int32)
    slot_of_item = (base + rank_table).reshape(-1).astype(jnp.int32)
    hits = rank_table[:, None, :] == places[None, :, None]
    item_of_slot = (base + lax.optimization_barrier(jnp.sum(jnp.where(hits, places[None, None, :], 0), axis=2))).reshape(-1).astype(jnp.int32)
    routed = encoded[item_of_slot]
    lengths = dec_len[item_of_slot]

    def whole(inputs_all, memory_all, stack, vector):

        def single(operands):
            return decode(operands[0], operands[1], operands[2], stack, vector)
        return lax.map(jax.checkpoint(single), (inputs_all, memory_all, lengths))
    results, backward = jax.vjp(whole, dec_in.astype(jnp.float32), routed, dec_stack, dec_vector)
    grad_inputs, grad_routed, grad_stack, grad_vector = backward(cotangent.astype(jnp.float32))
    grad_encoded = grad_routed[slot_of_item]
    return (results.astype(jnp.bfloat16), grad_inputs, grad_encoded, grad_stack, grad_vector)
```

```python
import functools

import jax
import jax.numpy as jnp
from jax import lax
from jax.experimental import pallas as pl
from jax.experimental.pallas import tpu as pltpu
from jax.sharding import PartitionSpec as P

D = 768
HEADS = 12
FF = 3072
PAIR = 128
BLOCK = 384
SCALE = 0.125
EPS = 1e-05
F32 = jnp.float32
BF16 = jnp.bfloat16
VMEM_LIMIT = 56 * 1024 * 1024
ANY = pl.BlockSpec(memory_space=pl.ANY)
VMEM = pl.BlockSpec(memory_space=pltpu.VMEM)
SMEM = pl.BlockSpec(memory_space=pltpu.SMEM)


def mm(left, right):
    return jnp.dot(left, right, preferred_element_type=F32)


def mm_t(left, right):
    return lax.dot_general(left, right, (((1,), (1,)), ((), ())), preferred_element_type=F32)


def t_mm(left, right):
    return lax.dot_general(left, right, (((0,), (0,)), ((), ())), preferred_element_type=F32)


def normed(values):
    mean = jnp.mean(values, axis=-1, keepdims=True)
    centred = values - mean
    root = lax.rsqrt(jnp.mean(centred * centred, axis=-1, keepdims=True) + EPS)
    return centred * root, root


def norm_back(unit, root, gain, grad):
    scaled = grad * gain
    first = jnp.mean(scaled, axis=-1, keepdims=True)
    second = jnp.mean(scaled * unit, axis=-1, keepdims=True)
    return root * (scaled - first - unit * second)


def col_sum(values):
    return jnp.sum(values, axis=0, keepdims=True)


def lane_low(rows):
    return lax.broadcasted_iota(jnp.int32, (rows, PAIR), 1) < PAIR // 2


def attend(q_ref, k_ref, v_ref, o_ref, p_ref, causal):
    rows = q_ref.shape[0]
    keys = k_ref.shape[0]
    low = lane_low(rows)
    if causal:
        keep = lax.broadcasted_iota(jnp.int32, (rows, keys), 0) >= lax.broadcasted_iota(
            jnp.int32, (rows, keys), 1
        )

    def pair(index, carry):
        cols = pl.ds(pl.multiple_of(index * PAIR, PAIR), PAIR)
        query = q_ref[:, cols]
        key = k_ref[:, cols]
        value = v_ref[:, cols]
        halves = []
        for half in range(2):
            mine = low if half == 0 else jnp.logical_not(low)
            scores = mm_t(jnp.where(mine, query, jnp.zeros_like(query)), key) * SCALE
            if causal:
                scores = jnp.where(keep, scores, -1e30)
            weights = jnp.exp(scores - jnp.max(scores, axis=-1, keepdims=True))
            inverse = 1.0 / jnp.sum(weights, axis=-1, keepdims=True)
            probs = (weights * inverse).astype(BF16)
            if p_ref is not None:
                p_ref[index * 2 + half] = probs
            halves.append(mm(probs, value))
        o_ref[:, cols] = jnp.where(low, halves[0], halves[1]).astype(BF16)
        return carry

    lax.fori_loop(0, HEADS // 2, pair, 0)


def attend_back(q_ref, k_ref, v_ref, o_ref, do_ref, p_ref, dq_ref, dk_ref, dv_ref):
    rows = q_ref.shape[0]
    low = lane_low(rows)

    def pair(index, carry):
        cols = pl.ds(pl.multiple_of(index * PAIR, PAIR), PAIR)
        query = q_ref[:, cols]
        key = k_ref[:, cols]
        value = v_ref[:, cols]
        grad = do_ref[:, cols]
        both = grad.astype(F32) * o_ref[:, cols].astype(F32)
        d_query = jnp.zeros((rows, PAIR), F32)
        d_key = jnp.zeros((rows, PAIR), F32)
        d_value = jnp.zeros((rows, PAIR), F32)
        for half in range(2):
            mine = low if half == 0 else jnp.logical_not(low)
            zero = jnp.zeros_like(query)
            grad_half = jnp.where(mine, grad, zero)
            delta = jnp.sum(jnp.where(mine, both, 0.0), axis=-1, keepdims=True)
            probs = p_ref[index * 2 + half]
            d_probs = mm_t(grad_half, value)
            d_scores = (probs.astype(F32) * (d_probs - delta)).astype(BF16)
            d_value += t_mm(probs, grad_half)
            d_query += mm(d_scores, jnp.where(mine, key, zero))
            d_key += t_mm(d_scores, jnp.where(mine, query, zero))
        dq_ref[:, cols] = (d_query * SCALE).astype(BF16)
        dk_ref[:, cols] = (d_key * SCALE).astype(BF16)
        dv_ref[:, cols] = d_value.astype(BF16)
        return carry

    lax.fori_loop(0, HEADS // 2, pair, 0)


def gelu_parts(values):
    upper = 0.5 * (1.0 + lax.erf(values * 0.7071067811865476))
    slope = upper + values * (0.3989422804014327 * jnp.exp(-0.5 * values * values))
    return values * upper, slope


def piece_copies(offs_ref, piece_refs, stack_ref, sems):
    copies = []
    for index, piece in enumerate(piece_refs):
        start = pl.multiple_of(offs_ref[index], 16)
        copy = pltpu.make_async_copy(
            piece, stack_ref.at[pl.ds(start, piece.shape[0])], sems.at[index]
        )
        copy.start()
        copies.append(copy)
    return copies


def enc_one(n, offs_ref, x_ref, vec_ref, *refs):
    pieces, (o_ref, rest_ref, w_ref, q_ref, k_ref, v_ref, sems, out_sem) = refs[:n], refs[n:]
    copies = piece_copies(offs_ref, pieces, w_ref, sems)
    unit, unused = normed(x_ref[...].astype(F32))
    a = (unit * vec_ref[0:1] + vec_ref[1:2]).astype(BF16)
    for copy in copies:
        copy.wait()
    spill = pltpu.make_async_copy(w_ref.at[pl.ds(3 * D, rest_ref.shape[0])], rest_ref, out_sem)
    spill.start()
    q_ref[...] = (mm(a, w_ref[0:D]) + vec_ref[4:5]).astype(BF16)
    k_ref[...] = mm(a, w_ref[D : 2 * D]).astype(BF16)
    v_ref[...] = (mm(a, w_ref[2 * D : 3 * D]) + vec_ref[5:6]).astype(BF16)
    attend(q_ref, k_ref, v_ref, o_ref, None, False)
    spill.wait()


def enc_two(x_ref, o_ref, vec_ref, w_ref, e_ref, acc_ref, m_ref):
    x2 = x_ref[...].astype(F32) + mm(o_ref[...], w_ref[0:D]) + vec_ref[6:7]
    unit, unused = normed(x2)
    m_ref[...] = (unit * vec_ref[2:3] + vec_ref[3:4]).astype(BF16)
    acc_ref[...] = x2 + vec_ref[7:8]

    def tile(j, carry):
        base = pl.multiple_of(j * D, D)
        u = mm_t(m_ref[...], w_ref[pl.ds(D + base, D)]) + vec_ref[pl.ds(8 + j, 1)]
        hid = (u * (0.5 * (1.0 + lax.erf(u * 0.7071067811865476)))).astype(BF16)
        acc_ref[...] += mm(hid, w_ref[pl.ds(D + FF + base, D)])
        return carry

    lax.fori_loop(0, FF // D, tile, 0)
    e_ref[...] = acc_ref[...].astype(BF16)


def dec_one(n, offs_ref, x_ref, vec_ref, *refs):
    pieces = refs[:n]
    q_ref, k_ref, v_ref, o_ref, p_ref, x2_ref = refs[n : n + 6]
    outs = refs[n + 6 : n + 9]
    w_ref, sems, out_sems = refs[n + 9 :]
    copies = piece_copies(offs_ref, pieces, w_ref, sems)
    x = x_ref[...].astype(F32)
    unit, unused = normed(x)
    a = (unit * vec_ref[0:1] + vec_ref[1:2]).astype(BF16)
    for copy in copies:
        copy.wait()
    spills = []
    first = 0
    for index, out in enumerate(outs):
        spills.append(
            pltpu.make_async_copy(
                w_ref.at[pl.ds(first, out.shape[0])], out, out_sems.at[index]
            )
        )
        first += out.shape[0]
        spills[-1].start()
    q_ref[...] = (mm(a, w_ref[0:D]) + vec_ref[6:7]).astype(BF16)
    k_ref[...] = mm(a, w_ref[D : 2 * D]).astype(BF16)
    v_ref[...] = (mm(a, w_ref[2 * D : 3 * D]) + vec_ref[7:8]).astype(BF16)
    attend(q_ref, k_ref, v_ref, o_ref, p_ref, True)
    x2_ref[...] = x + mm(o_ref[...], w_ref[3 * D : 4 * D]) + vec_ref[8:9]
    for spill in spills:
        spill.wait()


def dec_two(flag_ref, x2_ref, mine_ref, other_ref, vec_ref, w_ref, *refs):
    e_ref, q_ref, k_ref, v_ref, o_ref, p_ref, x3_ref = refs
    x2 = x2_ref[...]
    unit, unused = normed(x2)
    a = (unit * vec_ref[2:3] + vec_ref[3:4]).astype(BF16)

    @pl.when(flag_ref[0] == 1)
    def same():
        e_ref[...] = mine_ref[...]

    @pl.when(flag_ref[0] != 1)
    def swapped():
        e_ref[...] = other_ref[...]

    e = e_ref[...]
    q_ref[...] = (mm(a, w_ref[0:D]) + vec_ref[9:10]).astype(BF16)
    k_ref[...] = mm(e, w_ref[D : 2 * D]).astype(BF16)
    v_ref[...] = (mm(e, w_ref[2 * D : 3 * D]) + vec_ref[10:11]).astype(BF16)
    attend(q_ref, k_ref, v_ref, o_ref, p_ref, False)
    x3_ref[...] = x2 + mm(o_ref[...], w_ref[3 * D : 4 * D]) + vec_ref[11:12]


class Emitter:
    def __init__(self, slot_ref, out_ref, stage_ref, sems):
        self.slot_ref, self.out_ref, self.stage_ref, self.sems = slot_ref, out_ref, stage_ref, sems
        self.pending = [None, None]
        self.turn = 0

    def copies(self, place, first_block):
        result = []
        for part in range(2):
            slot = self.slot_ref[first_block + part]
            result.append(
                pltpu.make_async_copy(
                    self.stage_ref.at[place, pl.ds(part * BLOCK, BLOCK)],
                    self.out_ref.at[slot],
                    self.sems.at[place, part],
                )
            )
        return result

    def put(self, first_block, value):
        place = self.turn % 2
        if self.pending[place] is not None:
            for copy in self.pending[place]:
                copy.wait()
        self.stage_ref[place] = value.astype(BF16)
        self.pending[place] = self.copies(place, first_block)
        for copy in self.pending[place]:
            copy.start()
        self.turn += 1

    def finish(self):
        for pending in self.pending:
            if pending is not None:
                for copy in pending:
                    copy.wait()


def dec_three(slot_ref, len_ref, x3_ref, cot_ref, vec_ref, w_ref, *refs):
    y_ref, dx_ref, gv_ref, gw_ref = refs[:4]
    a_ref, rm_ref, acc_ref, da_ref, stage_ref, sems = refs[4:]
    rows = x3_ref.shape[0]
    live = (lax.broadcasted_iota(jnp.int32, (rows, 1), 0) < len_ref[0]).astype(F32)
    unit, root = normed(x3_ref[...])
    a_ref[...] = (unit * vec_ref[4:5] + vec_ref[5:6]).astype(BF16)
    rm = (live * cot_ref[...].astype(F32)).astype(BF16)
    rm_ref[...] = rm
    gv_ref[2:3] = col_sum(rm.astype(F32))
    emit = Emitter(slot_ref, gw_ref, stage_ref, sems)
    for j in range(FF // D):
        up = w_ref[j * D : (j + 1) * D]
        down = w_ref[FF + j * D : FF + (j + 1) * D]
        u = mm_t(a_ref[...], up) + vec_ref[13 + j : 14 + j]
        hidden, slope = gelu_parts(u)
        hid = hidden.astype(BF16)
        part = mm(hid, down)
        du_wide = slope * mm_t(rm_ref[...], down)
        du = du_wide.astype(BF16)
        gv_ref[3 + j : 4 + j] = col_sum(du.astype(F32))
        emit.put(24 + 2 * j, t_mm(hid, rm_ref[...]))
        emit.put(16 + 2 * j, t_mm(du, a_ref[...]))
        back = mm(du, up)
        if j == 0:
            acc_ref[...] = part
            da_ref[...] = back
        else:
            acc_ref[...] += part
            da_ref[...] += back
    y_ref[...] = (live * (x3_ref[...] + acc_ref[...] + vec_ref[12:13])).astype(BF16)
    grad = da_ref[...]
    unit, root = normed(x3_ref[...])
    gv_ref[0:1] = col_sum(grad * unit)
    gv_ref[1:2] = col_sum(grad)
    dy = live * cot_ref[...].astype(F32)
    dx_ref[...] = dy + norm_back(unit, root, vec_ref[4:5], grad)
    emit.finish()


def dec_four(slot_ref, dx3_ref, x2_ref, e_ref, q_ref, k_ref, v_ref, o_ref, p_ref, vec_ref, w_ref, *refs):
    unused, dx_ref, de_ref, gv_ref, gw_ref = refs[:5]
    do_ref, dq_ref, dk_ref, dv_ref, stage_ref, sems = refs[5:]
    emit = Emitter(slot_ref, gw_ref, stage_ref, sems)
    rc = dx3_ref[...].astype(BF16)
    gv_ref[2:3] = col_sum(rc.astype(F32))
    do_ref[...] = mm_t(rc, w_ref[3 * D : 4 * D]).astype(BF16)
    emit.put(14, t_mm(o_ref[...], rc))
    attend_back(q_ref, k_ref, v_ref, o_ref, do_ref, p_ref, dq_ref, dk_ref, dv_ref)
    unit, root = normed(x2_ref[...])
    a = (unit * vec_ref[2:3] + vec_ref[3:4]).astype(BF16)
    dq = dq_ref[...]
    dk = dk_ref[...]
    dv = dv_ref[...]
    gv_ref[3:4] = col_sum(dq.astype(F32))
    gv_ref[4:5] = col_sum(dv.astype(F32))
    de_ref[...] = mm_t(dk, w_ref[D : 2 * D]) + mm_t(dv, w_ref[2 * D : 3 * D])
    emit.put(8, t_mm(a, dq))
    emit.put(10, t_mm(e_ref[...], dk))
    emit.put(12, t_mm(e_ref[...], dv))
    grad = mm_t(dq, w_ref[0:D])
    gv_ref[0:1] = col_sum(grad * unit)
    gv_ref[1:2] = col_sum(grad)
    dx_ref[...] = dx3_ref[...] + norm_back(unit, root, vec_ref[2:3], grad)
    emit.finish()


def dec_five(slot_ref, dx2_ref, x_ref, q_ref, k_ref, v_ref, o_ref, p_ref, vec_ref, w_ref, *refs):
    unused, dx_ref, gv_ref, gw_ref = refs[:4]
    do_ref, dq_ref, dk_ref, dv_ref, stage_ref, sems = refs[4:]
    emit = Emitter(slot_ref, gw_ref, stage_ref, sems)
    rs = dx2_ref[...].astype(BF16)
    gv_ref[2:3] = col_sum(rs.astype(F32))
    do_ref[...] = mm_t(rs, w_ref[3 * D : 4 * D]).astype(BF16)
    emit.put(6, t_mm(o_ref[...], rs))
    attend_back(q_ref, k_ref, v_ref, o_ref, do_ref, p_ref, dq_ref, dk_ref, dv_ref)
    unit, root = normed(x_ref[...].astype(F32))
    a = (unit * vec_ref[0:1] + vec_ref[1:2]).astype(BF16)
    dq = dq_ref[...]
    dk = dk_ref[...]
    dv = dv_ref[...]
    gv_ref[3:4] = col_sum(dq.astype(F32))
    gv_ref[4:5] = col_sum(dv.astype(F32))
    emit.put(0, t_mm(a, dq))
    emit.put(2, t_mm(a, dk))
    emit.put(4, t_mm(a, dv))
    grad = mm_t(dq, w_ref[0:D]) + mm_t(dk, w_ref[D : 2 * D]) + mm_t(dv, w_ref[2 * D : 3 * D])
    gv_ref[0:1] = col_sum(grad * unit)
    gv_ref[1:2] = col_sum(grad)
    dx_ref[...] = dx2_ref[...] + norm_back(unit, root, vec_ref[0:1], grad)
    emit.finish()


def shaped(shape, dtype):
    return jax.ShapeDtypeStruct(shape, dtype)


def call(body, out_shape, in_specs, out_specs, scratch, aliases=()):
    return pl.pallas_call(
        body,
        out_shape=out_shape,
        in_specs=in_specs,
        out_specs=out_specs,
        scratch_shapes=scratch,
        input_output_aliases=dict(aliases),
        compiler_params=pltpu.CompilerParams(vmem_limit_bytes=VMEM_LIMIT),
    )


def run_encoder(frame, vec, offs, pieces):
    rows = frame.shape[0]
    n = len(pieces)
    total = 4 * D + 2 * FF
    act = shaped((rows, D), BF16)
    o, rest = call(
        functools.partial(enc_one, n),
        (act, shaped((total - 3 * D, D), BF16)),
        [SMEM, VMEM, VMEM] + [ANY] * n,
        (VMEM, ANY),
        [pltpu.VMEM((total, D), BF16)]
        + [pltpu.VMEM((rows, D), BF16)] * 3
        + [pltpu.SemaphoreType.DMA((n,)), pltpu.SemaphoreType.DMA],
    )(offs, frame, vec, *pieces)
    return call(
        enc_two,
        act,
        [VMEM] * 4,
        VMEM,
        [pltpu.VMEM((rows, D), F32), pltpu.VMEM((rows, D), BF16)],
    )(frame, o, vec, rest)


def run_decoder(x, cot, mine, other, flag, length, vec, offs, pieces, slots):
    rows = x.shape[0]
    n = len(pieces)
    total = 8 * D + 2 * FF
    act = shaped((rows, D), BF16)
    wide = shaped((rows, D), F32)
    probs = shaped((HEADS, rows, rows), BF16)
    attn = shaped((4 * D, D), BF16)
    q1, k1, v1, o1, p1, x2, w_self, w_cross, w_ff = call(
        functools.partial(dec_one, n),
        (act, act, act, act, probs, wide, attn, attn, shaped((2 * FF, D), BF16)),
        [SMEM, VMEM, VMEM] + [ANY] * n,
        (VMEM,) * 6 + (ANY,) * 3,
        [
            pltpu.VMEM((total, D), BF16),
            pltpu.SemaphoreType.DMA((n,)),
            pltpu.SemaphoreType.DMA((3,)),
        ],
    )(offs, x, vec, *pieces)
    e, q2, k2, v2, o2, p2, x3 = call(
        dec_two,
        (act, act, act, act, act, probs, wide),
        [SMEM] + [VMEM] * 5,
        (VMEM,) * 7,
        [],
    )(flag, x2, mine, other, vec, w_cross)
    blocks = shaped((total // BLOCK, BLOCK, D), BF16)
    stage = [pltpu.VMEM((2, D, D), BF16), pltpu.SemaphoreType.DMA((2, 2))]
    act_v = pltpu.VMEM((rows, D), BF16)
    wide_v = pltpu.VMEM((rows, D), F32)
    y, dx3, gv3, gw = call(
        dec_three,
        (act, wide, shaped((7, D), F32), blocks),
        [SMEM, SMEM] + [VMEM] * 4,
        (VMEM, VMEM, VMEM, ANY),
        [act_v, act_v, wide_v, wide_v] + stage,
    )(slots, length, x3, cot, vec, w_ff)
    dx2, de, gv2, gw = call(
        dec_four,
        (wide, wide, shaped((5, D), F32), blocks),
        [SMEM] + [VMEM] * 10 + [ANY],
        (VMEM, VMEM, VMEM, ANY),
        [act_v] * 4 + stage,
        aliases=((11, 3),),
    )(slots, dx3, x2, e, q2, k2, v2, o2, p2, vec, w_cross, gw)
    dx, gv1, gw = call(
        dec_five,
        (wide, shaped((5, D), F32), blocks),
        [SMEM] + [VMEM] * 9 + [ANY],
        (VMEM, VMEM, ANY),
        [act_v] * 4 + stage,
        aliases=((10, 2),),
    )(slots, dx2, x, q1, k1, v1, o1, p1, vec, w_self, gw)
    vec_rows = jnp.concatenate(
        [
            gv1[0:2],
            gv2[0:2],
            gv3[0:2],
            gv1[3:5],
            gv1[2:3],
            gv2[3:5],
            gv2[2:3],
            gv3[2:7],
        ],
        axis=0,
    )
    return y, dx, de, gw, vec_rows


AXES = ("wide", "narrow")


class Grid:
    def __init__(self):
        wide = lax.axis_size("wide")
        self.fits = wide == 16 and lax.axis_size("narrow") == 2
        self.wide = wide
        self.w = lax.axis_index("wide")
        self.y = lax.axis_index("narrow")

    def shift(self, value, step):
        n = self.wide
        return lax.ppermute(value, "wide", [(i, (i + 4 * step) % n) for i in range(n)])

    def x_swap(self, value):
        return lax.ppermute(value, "wide", [(i, i ^ 2) for i in range(self.wide)])

    def core_swap(self, value):
        return lax.ppermute(value, "wide", [(i, i ^ 1) for i in range(self.wide)])

    def y_swap(self, value):
        return lax.ppermute(value, "narrow", [(0, 1), (1, 0)])

    def flat(self, k, dx, dc, dy):
        z = (self.w // 4 + 4 - k) % 4
        x = ((self.w // 2) % 2) ^ dx
        c = (self.w % 2) ^ dc
        return (((z * 2 + x) * 2 + c) * 2 + (self.y ^ dy)).astype(jnp.int32)


barrier = lax.optimization_barrier
ORDER = [
    (1, 1, 1),
    (2, 1, 1),
    (3, 1, 0),
    (3, 1, 1),
    (2, 1, 0),
    (2, 0, 1),
    (2, 0, 0),
    (0, 1, 1),
    (3, 0, 1),
    (3, 0, 0),
    (1, 1, 0),
    (1, 0, 1),
    (0, 0, 1),
    (1, 0, 0),
    (0, 1, 0),
    (0, 0, 0),
]


def gather(grid, shard):
    rows = shard.shape[0]
    if not grid.fits:
        return [lax.all_gather(shard, AXES, axis=0, tiled=True)], jnp.zeros((1,), jnp.int32)
    a0 = shard
    x0, y0, a1 = barrier((grid.x_swap(a0), grid.y_swap(a0), grid.shift(a0, 1)))
    d0, y1, a2 = barrier((grid.x_swap(y0), grid.y_swap(a1), grid.shift(a1, 1)))
    x1, y2, a3 = barrier((grid.x_swap(a1), grid.y_swap(a2), grid.shift(a2, 1)))
    x2, y3, d1 = barrier((grid.x_swap(a2), grid.y_swap(a3), grid.shift(d0, 1)))
    x3, d2, d3 = barrier((grid.x_swap(a3), grid.y_swap(x2), grid.shift(d0, -1)))
    found = [
        ((0, 0, 0), a0), ((0, 1, 0), x0), ((0, 0, 1), y0), ((1, 0, 0), a1),
        ((0, 1, 1), d0), ((1, 0, 1), y1), ((2, 0, 0), a2),
        ((1, 1, 0), x1), ((2, 0, 1), y2), ((3, 0, 0), a3),
        ((2, 1, 0), x2), ((3, 0, 1), y3), ((1, 1, 1), d1),
        ((3, 1, 0), x3), ((2, 1, 1), d2), ((3, 1, 1), d3),
    ]
    pieces = []
    starts = []
    for (k, dx, dy), piece in found:
        pieces.append(piece)
        starts.append(grid.flat(k, dx, 0, dy) * rows)
    for (k, dx, dy), piece in found:
        pieces.append(grid.core_swap(piece))
        starts.append(grid.flat(k, dx, 1, dy) * rows)
    return pieces, jnp.stack(starts)


def gather_vectors(grid, enc, dec):
    if not grid.fits:
        return (
            lax.all_gather(enc, AXES, axis=0, tiled=True),
            lax.all_gather(dec, AXES, axis=0, tiled=True),
        )
    size = enc.shape[0] + dec.shape[0]
    row = jnp.concatenate([enc, dec])[None]
    rows = jnp.concatenate([row, grid.core_swap(row)], axis=0)
    rows = jnp.concatenate([rows, grid.x_swap(rows)], axis=0)
    rows = jnp.concatenate([rows, grid.y_swap(rows)], axis=0)
    planes = [rows]
    for unused in range(3):
        planes.append(grid.shift(planes[-1], 1))
    rows = jnp.concatenate(planes, axis=0)
    where = jnp.stack(
        [
            grid.flat(k, dx, dc, dy)
            for k in range(4)
            for dy in range(2)
            for dx in range(2)
            for dc in range(2)
        ]
    )
    pick = (jnp.arange(where.shape[0])[:, None] == where[None, :]).astype(BF16)
    ordered = mm(pick, rows)
    return ordered[:, : enc.shape[0]].reshape(-1), ordered[:, enc.shape[0] : size].reshape(-1)


def slot_table(grid, blocks):
    if not grid.fits:
        return jnp.arange(blocks, dtype=jnp.int32)
    places = [
        (grid.flat(k, dx, dc, dy), dc * 16 + index)
        for dc in range(2)
        for index, (k, dx, dy) in enumerate(ORDER)
    ]
    where = jnp.stack([f for f, unused in places])
    values = jnp.array([s for unused, s in places], jnp.int32)
    return jnp.sum(
        jnp.where(jnp.arange(blocks)[:, None] == where[None, :], values[None, :], 0), axis=1
    ).astype(jnp.int32)


def reduce_weights(grid, gw):
    if not grid.fits:
        return lax.psum_scatter(
            gw.reshape(-1, D), AXES, scatter_dimension=0, tiled=True
        ).astype(F32)
    came = []
    for part in range(4):
        came.append(grid.core_swap(gw[16 + 4 * part : 20 + 4 * part]))

    def term(k, dx, dy):
        index = ORDER.index((k, dx, dy))
        return gw[index].astype(F32) + came[index // 4][index % 4].astype(F32)

    def low(value):
        return value.astype(BF16)

    def up(value):
        return value.astype(F32)

    def total(key, *more):
        value = term(*key)
        for one in more:
            value = value + up(one)
        return value

    d1, d2, x3 = barrier(
        (
            grid.shift(low(total((1, 1, 1))), -1),
            grid.y_swap(low(total((2, 1, 1)))),
            grid.x_swap(low(total((3, 1, 0)))),
        )
    )
    d3, x2, y2 = barrier(
        (
            grid.shift(low(total((3, 1, 1))), 1),
            grid.x_swap(low(total((2, 1, 0), d2))),
            grid.y_swap(low(total((2, 0, 1)))),
        )
    )
    a2, d0, y3 = barrier(
        (
            grid.shift(low(total((2, 0, 0), x2, y2)), -1),
            grid.x_swap(low(total((0, 1, 1), d1, d3))),
            grid.y_swap(low(total((3, 0, 1)))),
        )
    )
    a3, x1, y1 = barrier(
        (
            grid.shift(low(total((3, 0, 0), x3, y3)), 1),
            grid.x_swap(low(total((1, 1, 0)))),
            grid.y_swap(low(total((1, 0, 1)))),
        )
    )
    a1, x0, y0 = barrier(
        (
            grid.shift(low(total((1, 0, 0), a2, x1, y1)), -1),
            grid.x_swap(low(total((0, 1, 0)))),
            grid.y_swap(low(total((0, 0, 1), d0))),
        )
    )
    return total((0, 0, 0), a1, a3, x0, y0)


def reduce_vectors(grid, rows):
    if not grid.fits:
        return lax.psum_scatter(rows.reshape(-1), AXES, scatter_dimension=0, tiled=True)
    rows = rows + grid.core_swap(rows)
    rows = rows + grid.x_swap(rows)
    rows = rows + grid.y_swap(rows)
    rows = rows + grid.shift(rows, 1)
    rows = rows + grid.shift(rows, 2)
    flat = rows.reshape(-1)
    size = flat.shape[0] // (grid.wide * 2)
    return lax.dynamic_slice_in_dim(flat, grid.flat(0, 0, 0, 0) * size, size)


def rank_within(buckets):
    places = jnp.arange(buckets.shape[0], dtype=jnp.int32)
    earlier = (buckets[None, :] < buckets[:, None]) | (
        (buckets[None, :] == buckets[:, None]) & (places[None, :] < places[:, None])
    )
    return jnp.sum(earlier.astype(jnp.int32), axis=1)


def per_device(
    frames, dec_in, cotangent, dec_len, bucket, enc_weights, enc_vectors, dec_weights, dec_vectors
):
    grid = Grid()
    members = lax.axis_size("narrow")
    wide_index = lax.axis_index("wide")
    narrow_index = lax.axis_index("narrow")
    group_buckets = lax.dynamic_slice_in_dim(bucket, wide_index * members, members)
    group_lengths = lax.dynamic_slice_in_dim(dec_len, wide_index * members, members)
    ranks = rank_within(group_buckets)
    places = jnp.arange(members, dtype=jnp.int32)
    chosen = ranks == narrow_index
    source = jnp.sum(jnp.where(chosen, places, 0))
    length = jnp.sum(jnp.where(chosen, group_lengths, 0))
    own_slot = jnp.sum(jnp.where(places == narrow_index, ranks, 0))

    enc_vec, dec_vec = gather_vectors(grid, enc_vectors, dec_vectors)
    enc_vec = enc_vec.astype(F32).reshape(-1, D)
    dec_vec = dec_vec.astype(F32).reshape(-1, D)
    enc_pieces, enc_offs = gather(grid, enc_weights)
    if grid.fits:
        dec_weights, enc_pieces = barrier((dec_weights, enc_pieces))
    dec_pieces, dec_offs = gather(grid, dec_weights)
    encoded = run_encoder(frames[0], enc_vec, enc_offs, enc_pieces)
    if members == 2:
        other = grid.y_swap(encoded)
    else:
        every = lax.all_gather(encoded, "narrow", axis=0)
        other = lax.dynamic_index_in_dim(every, source, keepdims=False)
    flag = (source == narrow_index).astype(jnp.int32)[None]
    slots = slot_table(grid, (8 * D + 2 * FF) // BLOCK)
    block_out, grad_inputs, grad_memory, grad_blocks, grad_rows = run_decoder(
        dec_in[0],
        cotangent[0],
        encoded,
        other,
        flag,
        length[None],
        dec_vec,
        dec_offs,
        dec_pieces,
        slots,
    )
    if members == 2:
        back = grid.y_swap(grad_memory.astype(BF16)).astype(F32)
    else:
        every = lax.all_gather(grad_memory.astype(BF16), "narrow", axis=0)
        back = lax.dynamic_index_in_dim(every, own_slot, keepdims=False).astype(F32)
    grad_encoded = jnp.where(own_slot == narrow_index, grad_memory, back)
    shard_stack = reduce_weights(grid, grad_blocks)
    shard_vector = reduce_vectors(grid, grad_rows)
    return (block_out[None], grad_inputs[None], grad_encoded[None], shard_stack, shard_vector)


def solution(mesh):
    items = P(AXES, None, None)
    rows = P(AXES, None)
    line = P(AXES)
    return jax.shard_map(
        per_device,
        mesh=mesh,
        in_specs=(items, items, items, P(), P(), rows, line, rows, line),
        out_specs=(items, items, items, rows, line),
        check_vma=False,
    )
```

```python
import functools

import jax
import jax.numpy as jnp
from jax import lax
from jax.experimental import pallas as pl
from jax.experimental.pallas import tpu as pltpu
from jax.sharding import PartitionSpec as P

D = 768
HEADS = 12
FF = 3072
PAIR = 128
BLOCK = 384
DEPTH = 4
SCALE = 0.125
EPS = 1e-05
F32 = jnp.float32
BF16 = jnp.bfloat16
VMEM_LIMIT = 56 * 1024 * 1024
ANY = pl.BlockSpec(memory_space=pl.ANY)
VMEM = pl.BlockSpec(memory_space=pltpu.VMEM)
SMEM = pl.BlockSpec(memory_space=pltpu.SMEM)


def mm(left, right):
    return jnp.dot(left, right, preferred_element_type=F32)


def mm_t(left, right):
    return lax.dot_general(left, right, (((1,), (1,)), ((), ())), preferred_element_type=F32)


def t_mm(left, right):
    return lax.dot_general(left, right, (((0,), (0,)), ((), ())), preferred_element_type=F32)


def normed(values):
    mean = jnp.mean(values, axis=-1, keepdims=True)
    centred = values - mean
    root = lax.rsqrt(jnp.mean(centred * centred, axis=-1, keepdims=True) + EPS)
    return centred * root, root


def norm_back(unit, root, gain, grad):
    scaled = grad * gain
    first = jnp.mean(scaled, axis=-1, keepdims=True)
    second = jnp.mean(scaled * unit, axis=-1, keepdims=True)
    return root * (scaled - first - unit * second)


def col_sum(values):
    return jnp.sum(values, axis=0, keepdims=True)


def lane_low(rows):
    return lax.broadcasted_iota(jnp.int32, (rows, PAIR), 1) < PAIR // 2


def attend(q_ref, k_ref, v_ref, o_ref, p_ref, causal):
    rows = q_ref.shape[0]
    keys = k_ref.shape[0]
    low = lane_low(rows)
    if causal:
        keep = lax.broadcasted_iota(jnp.int32, (rows, keys), 0) >= lax.broadcasted_iota(
            jnp.int32, (rows, keys), 1
        )

    def pair(index, carry):
        cols = pl.ds(pl.multiple_of(index * PAIR, PAIR), PAIR)
        query = q_ref[:, cols]
        key = k_ref[:, cols]
        value = v_ref[:, cols]
        halves = []
        for half in range(2):
            mine = low if half == 0 else jnp.logical_not(low)
            scores = mm_t(jnp.where(mine, query, jnp.zeros_like(query)), key) * SCALE
            if causal:
                scores = jnp.where(keep, scores, -1e30)
            weights = jnp.exp(scores - jnp.max(scores, axis=-1, keepdims=True))
            inverse = 1.0 / jnp.sum(weights, axis=-1, keepdims=True)
            probs = (weights * inverse).astype(BF16)
            if p_ref is not None:
                p_ref[index * 2 + half] = probs
            halves.append(mm(probs, value))
        o_ref[:, cols] = jnp.where(low, halves[0], halves[1]).astype(BF16)
        return carry

    lax.fori_loop(0, HEADS // 2, pair, 0)


def attend_back(q_ref, k_ref, v_ref, o_ref, do_ref, p_ref, dq_ref, dk_ref, dv_ref, wait):
    rows = q_ref.shape[0]
    low = lane_low(rows)

    def pair(index, carry):
        wait(index)
        cols = pl.ds(pl.multiple_of(index * PAIR, PAIR), PAIR)
        query = q_ref[:, cols]
        key = k_ref[:, cols]
        value = v_ref[:, cols]
        grad = do_ref[:, cols]
        both = grad.astype(F32) * o_ref[:, cols].astype(F32)
        d_query = jnp.zeros((rows, PAIR), F32)
        d_key = jnp.zeros((rows, PAIR), F32)
        d_value = jnp.zeros((rows, PAIR), F32)
        for half in range(2):
            mine = low if half == 0 else jnp.logical_not(low)
            zero = jnp.zeros_like(query)
            grad_half = jnp.where(mine, grad, zero)
            delta = jnp.sum(jnp.where(mine, both, 0.0), axis=-1, keepdims=True)
            probs = p_ref[index * 2 + half]
            d_probs = mm_t(grad_half, value)
            d_scores = (probs.astype(F32) * (d_probs - delta)).astype(BF16)
            d_value += t_mm(probs, grad_half)
            d_query += mm(d_scores, jnp.where(mine, key, zero))
            d_key += t_mm(d_scores, jnp.where(mine, query, zero))
        dq_ref[:, cols] = (d_query * SCALE).astype(BF16)
        dk_ref[:, cols] = (d_key * SCALE).astype(BF16)
        dv_ref[:, cols] = d_value.astype(BF16)
        return carry

    lax.fori_loop(0, HEADS // 2, pair, 0)


def gelu_parts(values):
    upper = 0.5 * (1.0 + lax.erf(values * 0.7071067811865476))
    slope = upper + values * (0.3989422804014327 * jnp.exp(-0.5 * values * values))
    return values * upper, slope


def piece_copies(offs_ref, piece_refs, stack_ref, sems):
    copies = []
    for index, piece in enumerate(piece_refs):
        start = pl.multiple_of(offs_ref[index], 16)
        copy = pltpu.make_async_copy(
            piece, stack_ref.at[pl.ds(start, piece.shape[0])], sems.at[index]
        )
        copy.start()
        copies.append(copy)
    return copies


def enc_one(n, offs_ref, x_ref, vec_ref, *refs):
    pieces, (q_ref, k_ref, v_ref, rest_ref, w_ref, sems, out_sem) = refs[:n], refs[n:]
    copies = piece_copies(offs_ref, pieces, w_ref, sems)
    unit, unused = normed(x_ref[...].astype(F32))
    a = (unit * vec_ref[0:1] + vec_ref[1:2]).astype(BF16)
    for copy in copies:
        copy.wait()
    spill = pltpu.make_async_copy(w_ref.at[pl.ds(3 * D, rest_ref.shape[0])], rest_ref, out_sem)
    spill.start()
    q_ref[...] = (mm(a, w_ref[0:D]) + vec_ref[4:5]).astype(BF16)
    k_ref[...] = mm(a, w_ref[D : 2 * D]).astype(BF16)
    v_ref[...] = (mm(a, w_ref[2 * D : 3 * D]) + vec_ref[5:6]).astype(BF16)
    spill.wait()


def enc_mid(q_ref, k_ref, v_ref, o_ref):
    attend(q_ref, k_ref, v_ref, o_ref, None, False)


def enc_two(x_ref, o_ref, vec_ref, w_ref, e_ref, acc_ref, m_ref):
    x2 = x_ref[...].astype(F32) + mm(o_ref[...], w_ref[0:D]) + vec_ref[6:7]
    unit, unused = normed(x2)
    m_ref[...] = (unit * vec_ref[2:3] + vec_ref[3:4]).astype(BF16)
    acc_ref[...] = x2 + vec_ref[7:8]

    def tile(j, carry):
        base = pl.multiple_of(j * D, D)
        u = mm_t(m_ref[...], w_ref[pl.ds(D + base, D)]) + vec_ref[pl.ds(8 + j, 1)]
        hid = (u * (0.5 * (1.0 + lax.erf(u * 0.7071067811865476)))).astype(BF16)
        acc_ref[...] += mm(hid, w_ref[pl.ds(D + FF + base, D)])
        return carry

    lax.fori_loop(0, FF // D, tile, 0)
    e_ref[...] = acc_ref[...].astype(BF16)


class Loader:
    def __init__(self, sems):
        self.sems = sems
        self.count = 0

    def start(self, source, target):
        copy = pltpu.make_async_copy(source, target, self.sems.at[self.count])
        copy.start()
        self.count += 1
        return copy

    def heads(self, source, target):
        first = self.count
        for index in range(HEADS // 2):
            self.start(source.at[pl.ds(2 * index, 2)], target.at[pl.ds(2 * index, 2)])

        def wait(index):
            pltpu.make_async_copy(
                source.at[pl.ds(2 * index, 2)], target.at[pl.ds(2 * index, 2)], self.sems.at[first + index]
            ).wait()

        return wait


class Saver:
    def __init__(self, left_ref, right_ref, sems):
        self.left_ref, self.right_ref, self.sems = left_ref, right_ref, sems
        self.started = []

    def start(self, source, target):
        copy = pltpu.make_async_copy(source, target, self.sems.at[len(self.started)])
        copy.start()
        self.started.append(copy)

    def left(self, first, ref):
        for part in range(ref.shape[1] // BLOCK):
            self.start(ref.at[:, pl.ds(part * BLOCK, BLOCK)], self.left_ref.at[first + part])

    def right(self, place, ref):
        self.start(ref, self.right_ref.at[place])

    def finish(self):
        for copy in self.started:
            copy.wait()


def dec_one(n, offs_ref, x_ref, vec_ref, *refs):
    pieces, refs = refs[:n], refs[n:]
    q_ref, k_ref, v_ref, o_ref, p_ref, x2_ref = refs[:6]
    outs, left_ref = refs[6:9], refs[9]
    w_ref, a_ref, sems, out_sems, save_sems = refs[10:]
    save = Saver(left_ref, None, save_sems)
    rows = pieces[0].shape[0]
    for index, piece in enumerate(pieces):
        start = pl.multiple_of(offs_ref[index], 16)
        place = lax.div(offs_ref[index], rows) if n > 1 else 0
        pltpu.make_async_copy(piece, w_ref.at[pl.ds(start, rows)], sems.at[place]).start()

    def arrived(first, last):
        if n > 1:
            for place in range(first // rows, last // rows):
                pltpu.make_async_copy(
                    pieces[0], w_ref.at[pl.ds(place * rows, rows)], sems.at[place]
                ).wait()
        elif first == 0:
            pltpu.make_async_copy(pieces[0], w_ref, sems.at[0]).wait()

    x = x_ref[...].astype(F32)
    unit, unused = normed(x)
    a_ref[...] = (unit * vec_ref[0:1] + vec_ref[1:2]).astype(BF16)
    save.left(0, a_ref)
    arrived(0, 4 * D)
    q_ref[...] = (mm(a_ref[...], w_ref[0:D]) + vec_ref[6:7]).astype(BF16)
    k_ref[...] = mm(a_ref[...], w_ref[D : 2 * D]).astype(BF16)
    v_ref[...] = (mm(a_ref[...], w_ref[2 * D : 3 * D]) + vec_ref[7:8]).astype(BF16)
    arrived(4 * D, 8 * D + 2 * FF)
    spills = []
    first = 0
    for index, out in enumerate(outs):
        spills.append(
            pltpu.make_async_copy(w_ref.at[pl.ds(first, out.shape[0])], out, out_sems.at[index])
        )
        spills[-1].start()
        first += out.shape[0]
    attend(q_ref, k_ref, v_ref, o_ref, p_ref, True)
    save.left(2, o_ref)
    x2_ref[...] = x + mm(o_ref[...], w_ref[3 * D : 4 * D]) + vec_ref[8:9]
    for copy in spills:
        copy.wait()
    save.finish()


def dec_two(flag_ref, x2_ref, mine_ref, other_ref, vec_ref, w_hbm, unused_ref, *refs):
    q_ref, k_ref, v_ref, o_ref, p_ref, x3_ref, left_ref = refs[:7]
    w_ref, a_ref, e_ref, sems, save_sems = refs[7:]
    save = Saver(left_ref, None, save_sems)
    load = Loader(sems)
    weights = [
        load.start(w_hbm.at[pl.ds(first * D, D)], w_ref.at[pl.ds(first * D, D)]) for first in range(4)
    ]

    @pl.when(flag_ref[0] == 1)
    def same():
        e_ref[...] = mine_ref[...]

    @pl.when(flag_ref[0] != 1)
    def swapped():
        e_ref[...] = other_ref[...]

    unit, unused = normed(x2_ref[...])
    a_ref[...] = (unit * vec_ref[2:3] + vec_ref[3:4]).astype(BF16)
    save.left(6, e_ref)
    save.left(4, a_ref)
    weights[0].wait()
    q_ref[...] = (mm(a_ref[...], w_ref[0:D]) + vec_ref[9:10]).astype(BF16)
    weights[1].wait()
    k_ref[...] = mm(e_ref[...], w_ref[D : 2 * D]).astype(BF16)
    weights[2].wait()
    v_ref[...] = (mm(e_ref[...], w_ref[2 * D : 3 * D]) + vec_ref[10:11]).astype(BF16)
    attend(q_ref, k_ref, v_ref, o_ref, p_ref, False)
    save.left(8, o_ref)
    weights[3].wait()
    x3_ref[...] = x2_ref[...] + mm(o_ref[...], w_ref[3 * D : 4 * D]) + vec_ref[11:12]
    save.finish()


def dec_three(len_ref, x3_ref, cot_ref, vec_ref, w_hbm, *refs):
    y_ref, dx_ref, gv_ref, left_ref, right_ref = refs[:5]
    w_ref, a_ref, rm_ref, hid_ref, du_ref, acc_ref, da_ref, sems, save_sems = refs[5:]
    save = Saver(left_ref, right_ref, save_sems)
    load = Loader(sems)
    tiles = []
    for j in range(FF // D):
        for first in (j * D, FF + j * D):
            tiles.append(load.start(w_hbm.at[pl.ds(first, D)], w_ref.at[pl.ds(first, D)]))
    rows = x3_ref.shape[0]
    live = (lax.broadcasted_iota(jnp.int32, (rows, 1), 0) < len_ref[0]).astype(F32)
    unit, root = normed(x3_ref[...])
    a_ref[...] = (unit * vec_ref[4:5] + vec_ref[5:6]).astype(BF16)
    rm = (live * cot_ref[...].astype(F32)).astype(BF16)
    rm_ref[...] = rm
    save.right(0, a_ref)
    save.right(1, rm_ref)
    gv_ref[2:3] = col_sum(rm.astype(F32))
    for j in range(FF // D):
        tiles[2 * j].wait()
        tiles[2 * j + 1].wait()
        down = w_ref[FF + j * D : FF + (j + 1) * D]
        up = w_ref[j * D : (j + 1) * D]
        u = mm_t(a_ref[...], up) + vec_ref[13 + j : 14 + j]
        hidden, slope = gelu_parts(u)
        hid = hidden.astype(BF16)
        part = mm(hid, down)
        du_wide = slope * mm_t(rm_ref[...], down)
        du = du_wide.astype(BF16)
        gv_ref[3 + j : 4 + j] = col_sum(du.astype(F32))
        hid_ref[j] = hid
        du_ref[j] = du
        save.left(2 * j, du_ref.at[j])
        save.left(8 + 2 * j, hid_ref.at[j])
        back = mm(du, up)
        if j == 0:
            acc_ref[...] = part
            da_ref[...] = back
        else:
            acc_ref[...] += part
            da_ref[...] += back
    y_ref[...] = (live * (x3_ref[...] + acc_ref[...] + vec_ref[12:13])).astype(BF16)
    grad = da_ref[...]
    unit, root = normed(x3_ref[...])
    gv_ref[0:1] = col_sum(grad * unit)
    gv_ref[1:2] = col_sum(grad)
    dy = live * cot_ref[...].astype(F32)
    dx_ref[...] = dy + norm_back(unit, root, vec_ref[4:5], grad)
    save.finish()


def dec_four(dx3_ref, vec_ref, x2_hbm, q_hbm, k_hbm, v_hbm, o_hbm, p_hbm, w_hbm, *refs):
    dx_ref, de_ref, gv_ref, right_ref = refs[:4]
    r_ref, s_ref, do_ref, dq_ref, dk_ref, dv_ref = refs[4:10]
    x2_ref, q_ref, k_ref, v_ref, o_ref, p_ref, w_ref, sems, save_sems = refs[10:]
    save = Saver(None, right_ref, save_sems)
    load = Loader(sems)
    out_weights = load.start(w_hbm.at[pl.ds(3 * D, D)], w_ref.at[pl.ds(3 * D, D)])
    operands = [
        load.start(source, target)
        for source, target in ((q_hbm, q_ref), (k_hbm, k_ref), (v_hbm, v_ref), (o_hbm, o_ref))
    ]
    wait = load.heads(p_hbm, p_ref)
    rest = [
        load.start(w_hbm.at[pl.ds(0, 3 * D)], w_ref.at[pl.ds(0, 3 * D)]),
        load.start(x2_hbm, x2_ref),
    ]
    rc = dx3_ref[...].astype(BF16)
    r_ref[...] = rc
    save.right(3, r_ref)
    gv_ref[2:3] = col_sum(rc.astype(F32))
    out_weights.wait()
    do_ref[...] = mm_t(r_ref[...], w_ref[3 * D : 4 * D]).astype(BF16)
    for copy in operands:
        copy.wait()
    attend_back(q_ref, k_ref, v_ref, o_ref, do_ref, p_ref, dq_ref, dk_ref, dv_ref, wait)
    save.right(0, dq_ref)
    save.right(1, dk_ref)
    save.right(2, dv_ref)
    for copy in rest:
        copy.wait()
    grad = mm_t(dq_ref[...], w_ref[0:D])
    unit, root = normed(x2_ref[...])
    gv_ref[0:1] = col_sum(grad * unit)
    gv_ref[1:2] = col_sum(grad)
    dx = dx3_ref[...] + norm_back(unit, root, vec_ref[2:3], grad)
    dx_ref[...] = dx
    s_ref[...] = dx.astype(BF16)
    save.right(4, s_ref)
    dq = dq_ref[...]
    dk = dk_ref[...]
    dv = dv_ref[...]
    gv_ref[3:4] = col_sum(dq.astype(F32))
    gv_ref[4:5] = col_sum(dv.astype(F32))
    de_ref[...] = mm_t(dk, w_ref[D : 2 * D]) + mm_t(dv, w_ref[2 * D : 3 * D])
    save.finish()


def dec_five(dx2_ref, q_hbm, k_hbm, v_hbm, o_hbm, p_hbm, w_hbm, right_ref, *refs):
    do_ref, q_ref, k_ref, v_ref, o_ref, p_ref, w_ref, sems = refs
    load = Loader(sems)
    out_weights = load.start(w_hbm.at[pl.ds(3 * D, D)], w_ref)
    operands = [
        load.start(source, target)
        for source, target in ((q_hbm, q_ref), (k_hbm, k_ref), (v_hbm, v_ref), (o_hbm, o_ref))
    ]
    wait = load.heads(p_hbm, p_ref)
    rs = dx2_ref[...].astype(BF16)
    out_weights.wait()
    do_ref[...] = mm_t(rs, w_ref[...]).astype(BF16)
    for copy in operands:
        copy.wait()
    attend_back(
        q_ref, k_ref, v_ref, o_ref, do_ref, p_ref, right_ref.at[0], right_ref.at[1], right_ref.at[2], wait
    )


def dec_six(dx2_ref, x_ref, right_ref, vec_ref, w_ref, gv3_ref, gv2_ref, dx_ref, gv_ref):
    dq = right_ref[0]
    dk = right_ref[1]
    dv = right_ref[2]
    grad = mm_t(dq, w_ref[0:D]) + mm_t(dk, w_ref[D : 2 * D]) + mm_t(dv, w_ref[2 * D : 3 * D])
    unit, root = normed(x_ref[...].astype(F32))
    gv_ref[0:1] = col_sum(grad * unit)
    gv_ref[1:2] = col_sum(grad)
    gv_ref[2:4] = gv2_ref[0:2]
    gv_ref[4:6] = gv3_ref[0:2]
    gv_ref[6:7] = col_sum(dq.astype(F32))
    gv_ref[7:8] = col_sum(dv.astype(F32))
    gv_ref[8:9] = col_sum(dx2_ref[...].astype(BF16).astype(F32))
    gv_ref[9:11] = gv2_ref[3:5]
    gv_ref[11:12] = gv2_ref[2:3]
    gv_ref[12:17] = gv3_ref[2:7]
    dx_ref[...] = dx2_ref[...] + norm_back(unit, root, vec_ref[0:1], grad)


def weight_blocks(count, sides, id_ref, left_id_ref, right_id_ref, *refs):
    groups = [refs[sides * g : sides * g + sides] for g in range(5)]
    lefts_a, lefts_f, rights_f, rights_c, rights_s = groups
    refs = refs[5 * sides :]
    outs = refs[:count]
    left_ref, right_ref, stage_ref, sems, out_sems = refs[count:]

    def fetch(i):
        place = i % DEPTH
        block = id_ref[i]

        def start(lefts, rights):
            for side in range(sides):
                pltpu.make_async_copy(
                    lefts[side].at[left_id_ref[block]], left_ref.at[place, side], sems.at[place, 0, side]
                ).start()
                pltpu.make_async_copy(
                    rights[side].at[right_id_ref[block]], right_ref.at[place, side], sems.at[place, 1, side]
                ).start()

        @pl.when(block < 6)
        def own_attention():
            start(lefts_a, rights_s)

        @pl.when(jnp.logical_and(block >= 6, block < 16))
        def cross_attention():
            start(lefts_a, rights_c)

        @pl.when(block >= 16)
        def feed_forward():
            start(lefts_f, rights_f)

    def ended(i):
        place = i % DEPTH
        for side in range(sides):
            pltpu.make_async_copy(
                lefts_a[0].at[0], left_ref.at[place, side], sems.at[place, 0, side]
            ).wait()
            pltpu.make_async_copy(
                rights_f[0].at[0], right_ref.at[place, side], sems.at[place, 1, side]
            ).wait()

    rows = left_ref.shape[2]
    for i in range(min(DEPTH - 1, count)):
        fetch(i)
    sent = [None, None]
    for i in range(count):
        if i + DEPTH - 1 < count:
            fetch(i + DEPTH - 1)
        ended(i)
        place = i % DEPTH
        value = t_mm(
            left_ref[place].reshape(sides * rows, BLOCK), right_ref[place].reshape(sides * rows, D)
        )
        place = i % 2
        if sent[place] is not None:
            sent[place].wait()
        stage_ref[place] = value.astype(BF16)
        sent[place] = pltpu.make_async_copy(stage_ref.at[place], outs[i], out_sems.at[place])
        sent[place].start()
    for copy in sent:
        if copy is not None:
            copy.wait()


def shaped(shape, dtype):
    return jax.ShapeDtypeStruct(shape, dtype)


def call(body, out_shape, in_specs, out_specs, scratch, micros, aliases=()):
    return pl.pallas_call(
        body,
        out_shape=out_shape,
        in_specs=in_specs,
        out_specs=out_specs,
        scratch_shapes=scratch,
        input_output_aliases=dict(aliases),
        cost_estimate=pl.CostEstimate(
            flops=int(micros * 1e9), bytes_accessed=int(micros * 1e5), transcendentals=0
        ),
        compiler_params=pltpu.CompilerParams(vmem_limit_bytes=VMEM_LIMIT),
    )


def encoder_parts(frame, vec, offs, pieces):
    rows = frame.shape[0]
    n = len(pieces)
    total = 4 * D + 2 * FF
    act = shaped((rows, D), BF16)

    def first():
        return call(
            functools.partial(enc_one, n),
            (act, act, act, shaped((total - 3 * D, D), BF16)),
            [SMEM, VMEM, VMEM] + [ANY] * n,
            (VMEM, VMEM, VMEM, ANY),
            [
                pltpu.VMEM((total, D), BF16),
                pltpu.SemaphoreType.DMA((n,)),
                pltpu.SemaphoreType.DMA,
            ],
            9,
        )(offs, frame, vec, *pieces)

    def second(q, k, v):
        return call(enc_mid, act, [VMEM] * 3, VMEM, [], 10)(q, k, v)

    def third(o, rest):
        return call(
            enc_two,
            act,
            [VMEM] * 4,
            VMEM,
            [pltpu.VMEM((rows, D), F32), pltpu.VMEM((rows, D), BF16)],
            12,
        )(frame, o, vec, rest)

    return first, second, third


def run_decoder(x, cot, mine, other, flag, length, vec, offs, pieces, swap):
    rows = x.shape[0]
    n = len(pieces)
    total = 8 * D + 2 * FF
    act = shaped((rows, D), BF16)
    wide = shaped((rows, D), F32)
    probs = shaped((HEADS, rows, rows), BF16)
    attn = shaped((4 * D, D), BF16)
    lefts = shaped((10, rows, BLOCK), BF16)
    act_v = pltpu.VMEM((rows, D), BF16)
    wide_v = pltpu.VMEM((rows, D), F32)
    half_v = pltpu.VMEM((FF // D, rows, D), BF16)

    def sems(count):
        return pltpu.SemaphoreType.DMA((count,))

    probs_v = pltpu.VMEM((HEADS, rows, rows), BF16)
    half = (act, act, act, act, probs, wide)
    q1, k1, v1, o1, p1, x2, w_self, w_cross, w_ff, left_a = call(
        functools.partial(dec_one, n),
        half + (attn, attn, shaped((2 * FF, D), BF16), lefts),
        [SMEM, VMEM, VMEM] + [ANY] * n,
        (VMEM,) * 6 + (ANY,) * 4,
        [pltpu.VMEM((total, D), BF16), act_v, sems(n), sems(3), sems(4)],
        17,
    )(offs, x, vec, *pieces)
    q2, k2, v2, o2, p2, x3, left_a = call(
        dec_two,
        half + (lefts,),
        [SMEM] + [VMEM] * 4 + [ANY] * 2,
        (VMEM,) * 6 + (ANY,),
        [pltpu.VMEM((4 * D, D), BF16), act_v, act_v, sems(4), sems(6)],
        15,
        aliases=((6, 6),),
    )(flag, x2, mine, other, vec, w_cross, left_a)
    left_a_other = swap(left_a)
    y, dx3, gv3, left_f, right_f = call(
        dec_three,
        (
            act,
            wide,
            shaped((7, D), F32),
            shaped((16, rows, BLOCK), BF16),
            shaped((2, rows, D), BF16),
        ),
        [SMEM] + [VMEM] * 3 + [ANY],
        (VMEM, VMEM, VMEM, ANY, ANY),
        [pltpu.VMEM((2 * FF, D), BF16), act_v, act_v, half_v, half_v, wide_v, wide_v]
        + [sems(8), sems(18)],
        15,
    )(length, x3, cot, vec, w_ff)
    left_f_other = swap(left_f)
    right_f_other = swap(right_f)
    dx2, de, gv2, right_c = call(
        dec_four,
        (wide, wide, shaped((5, D), F32), shaped((5, rows, D), BF16)),
        [VMEM] * 2 + [ANY] * 7,
        (VMEM, VMEM, VMEM, ANY),
        [act_v] * 6
        + [wide_v, act_v, act_v, act_v, act_v, probs_v, pltpu.VMEM((4 * D, D), BF16)]
        + [sems(13), sems(5)],
        16,
    )(dx3, vec, x2, q2, k2, v2, o2, p2, w_cross)
    right_c_other = swap(right_c)
    right_s = call(
        dec_five,
        shaped((3, rows, D), BF16),
        [VMEM] + [ANY] * 6,
        VMEM,
        [act_v] * 5 + [probs_v, pltpu.VMEM((D, D), BF16), sems(11)],
        12,
    )(dx2, q1, k1, v1, o1, p1, w_self)
    right_s_other = swap(right_s)
    dx, vec_rows = call(
        dec_six,
        (wide, shaped((17, D), F32)),
        [VMEM] * 7,
        (VMEM, VMEM),
        [],
        5,
    )(dx2, x, right_s, vec, w_self, gv3, gv2)
    saved = [
        (left_a, left_a_other),
        (left_f, left_f_other),
        (right_f, right_f_other),
        (right_c, right_c_other),
        (right_s, right_s_other),
    ]
    return y, dx, de, saved, vec_rows


LEFT_OF = [0, 1, 0, 1, 0, 1, 2, 3, 4, 5, 6, 7, 6, 7, 8, 9] + list(range(16))
RIGHT_OF = [0, 0, 1, 1, 2, 2, 4, 4] + [0, 0, 1, 1, 2, 2, 3, 3] + [0] * 8 + [1] * 8


def gradient_blocks(saved, blocks, sides):
    count = blocks.shape[0]
    rows = saved[0][0].shape[1]
    given = [value for pair in saved for value in pair[:sides]]
    return call(
        functools.partial(weight_blocks, count, sides),
        (shaped((BLOCK, D), BF16),) * count,
        [SMEM] * 3 + [ANY] * len(given),
        (ANY,) * count,
        [
            pltpu.VMEM((DEPTH, sides, rows, BLOCK), BF16),
            pltpu.VMEM((DEPTH, sides, rows, D), BF16),
            pltpu.VMEM((2, BLOCK, D), BF16),
            pltpu.SemaphoreType.DMA((DEPTH, 2, sides)),
            pltpu.SemaphoreType.DMA((2,)),
        ],
        count,
    )(blocks, jnp.array(LEFT_OF, jnp.int32), jnp.array(RIGHT_OF, jnp.int32), *given)


AXES = ("wide", "narrow")


class Grid:
    def __init__(self):
        wide = lax.axis_size("wide")
        self.fits = wide == 16 and lax.axis_size("narrow") == 2
        self.wide = wide
        self.w = lax.axis_index("wide")
        self.y = lax.axis_index("narrow")
        self.last = {}

    def send(self, link, value, after=()):
        line = link[0]
        before = tuple(after) + ((self.last[line],) if line in self.last else ())
        if before:
            value = barrier((value,) + before)[0]
        if link == "x":
            came = self.x_swap(value)
        elif link == "y":
            came = self.y_swap(value)
        else:
            came = self.shift(value, 1 if link == "z+" else -1)
        self.last[line] = came
        return came

    def shift(self, value, step):
        n = self.wide
        return lax.ppermute(value, "wide", [(i, (i + 4 * step) % n) for i in range(n)])

    def x_swap(self, value):
        return lax.ppermute(value, "wide", [(i, i ^ 2) for i in range(self.wide)])

    def core_swap(self, value):
        return lax.ppermute(value, "wide", [(i, i ^ 1) for i in range(self.wide)])

    def y_swap(self, value):
        return lax.ppermute(value, "narrow", [(0, 1), (1, 0)])

    def flat(self, k, dx, dc, dy):
        z = (self.w // 4 + 4 - k) % 4
        x = ((self.w // 2) % 2) ^ dx
        c = (self.w % 2) ^ dc
        return (((z * 2 + x) * 2 + c) * 2 + (self.y ^ dy)).astype(jnp.int32)


barrier = lax.optimization_barrier
STEPS = [
    ("a1", "z+", "a0"), ("x0", "x", "a0"), ("y0", "y", "a0"),
    ("a3", "z-", "a0"), ("x1", "x", "a1"), ("y1", "y", "a1"),
    ("a2", "z+", "a1"), ("d0", "x", "y0"), ("y3", "y", "a3"),
    ("d1", "z+", "d0"), ("x2", "x", "a2"), ("y2", "y", "a2"),
    ("d3", "z-", "d0"), ("x3", "x", "a3"), ("d2", "y", "x2"),
]
KEYS = {
    kind + str(k): (k, int(kind in "xd"), int(kind in "yd")) for kind in "axyd" for k in range(4)
}


def gather(grid, shard, hooks):
    rows = shard.shape[0]
    if not grid.fits:
        return [lax.all_gather(shard, AXES, axis=0, tiled=True)], jnp.zeros((1,), jnp.int32)
    got = {"a0": shard}
    after = []
    for slot in range(5):
        ended = [got[name] for name, unused, unused in STEPS[3 * slot - 3 : 3 * slot]] if slot else []
        after.append(hooks[slot](ended) if slot < len(hooks) else ())
        for name, link, source in STEPS[3 * slot : 3 * slot + 3]:
            got[name] = grid.send(link, got[source], after[slot - 1] if slot else ())
    found = [(KEYS[name], got[name]) for name in got]
    pieces = []
    starts = []
    for (k, dx, dy), piece in found:
        pieces.append(piece)
        starts.append(grid.flat(k, dx, 0, dy) * rows)
    for (k, dx, dy), piece in found:
        pieces.append(grid.core_swap(piece))
        starts.append(grid.flat(k, dx, 1, dy) * rows)
    return pieces, jnp.stack(starts)


def vector_hooks(grid, enc, dec, found):
    held = [jnp.concatenate([enc, dec])[None]]

    def step(swap):
        def hook(ended):
            rows = held[-1]
            if ended:
                rows = barrier((rows,) + tuple(ended))[0]
            came = swap(rows)
            held.append(jnp.concatenate([held[-1], came], axis=0))
            return (came,)

        return hook

    def planes(ended):
        rows = barrier((held[-1],) + tuple(ended))[0]
        came = [grid.shift(rows, step) for step in (1, 2, 3)]
        found.append(jnp.concatenate([held[-1]] + came, axis=0))
        return tuple(came)

    return [step(grid.core_swap), step(grid.x_swap), step(grid.y_swap), planes]


def gather_vectors(grid, enc, dec, found):
    if not grid.fits:
        return (
            lax.all_gather(enc, AXES, axis=0, tiled=True),
            lax.all_gather(dec, AXES, axis=0, tiled=True),
        )
    size = enc.shape[0] + dec.shape[0]
    rows = found[0]
    where = jnp.stack(
        [
            grid.flat(k, dx, dc, dy)
            for k in range(4)
            for dy in range(2)
            for dx in range(2)
            for dc in range(2)
        ]
    )
    pick = (jnp.arange(where.shape[0])[:, None] == where[None, :]).astype(BF16)
    ordered = mm(pick, rows)
    return ordered[:, : enc.shape[0]].reshape(-1), ordered[:, enc.shape[0] : size].reshape(-1)


def reduce_weights(grid, saved, hooks):
    if not grid.fits:
        blocks = gradient_blocks(saved, jnp.arange(len(LEFT_OF), dtype=jnp.int32), 1)
        return lax.psum_scatter(
            jnp.concatenate(blocks, axis=0), AXES, scatter_dimension=0, tiled=True
        ).astype(F32)
    terms = {}

    def prepare(keys, ended=()):
        blocks = jnp.stack([grid.flat(k, dx, 0, dy) for k, dx, dy in keys])
        if ended:
            blocks = barrier((blocks,) + tuple(ended))[0]
        for key, block in zip(keys, gradient_blocks(saved, blocks, 2)):
            terms[key] = block

    def term(key):
        return terms[key].astype(F32)

    def low(value):
        return value.astype(BF16)

    def up(value):
        return value.astype(F32)

    def total(key, *more):
        value = term(key)
        for one in more:
            value = value + up(one)
        return value

    held = {name: [] for name in KEYS}
    back = {"x": "x", "y": "y", "z+": "z-", "z-": "z+"}
    order = list(reversed(STEPS))
    after = []
    came_last = []
    keys = [KEYS[name] for name, unused, unused in order] + [KEYS["a0"]]
    prepare(keys[:3])
    prepare(keys[3:8])
    for slot in range(5):
        after.append(hooks[slot](came_last) if slot < len(hooks) else ())
        if slot == 1:
            prepare(keys[8:], came_last)
        came_last = []
        for name, link, target in order[3 * slot : 3 * slot + 3]:
            came_last.append(
                grid.send(
                    back[link],
                    low(total(KEYS[name], *held[name])),
                    after[slot - 1] if slot else (),
                )
            )
            held[target].append(came_last[-1])
    most = barrier((total(KEYS["a0"], *held["a0"][:-1]),))[0]
    return most + up(held["a0"][-1])


def sum_hooks(grid, held):
    def step(swap):
        def hook(ended):
            rows = held[-1]
            if ended:
                rows = barrier((rows,) + tuple(ended))[0]
            held.append(held[-1] + swap(rows))
            return (held[-1],)

        return hook

    return [
        step(grid.core_swap),
        step(grid.x_swap),
        step(grid.y_swap),
        step(lambda rows: grid.shift(rows, 1)),
        step(lambda rows: grid.shift(rows, 2)),
    ]


def own_vectors(grid, rows):
    if not grid.fits:
        return lax.psum_scatter(rows.reshape(-1), AXES, scatter_dimension=0, tiled=True)
    flat = rows.reshape(-1)
    size = flat.shape[0] // (grid.wide * 2)
    return lax.dynamic_slice_in_dim(flat, grid.flat(0, 0, 0, 0) * size, size)


def rank_within(buckets):
    places = jnp.arange(buckets.shape[0], dtype=jnp.int32)
    earlier = (buckets[None, :] < buckets[:, None]) | (
        (buckets[None, :] == buckets[:, None]) & (places[None, :] < places[:, None])
    )
    return jnp.sum(earlier.astype(jnp.int32), axis=1)


def per_device(
    frames, dec_in, cotangent, dec_len, bucket, enc_weights, enc_vectors, dec_weights, dec_vectors
):
    grid = Grid()
    members = lax.axis_size("narrow")
    wide_index = lax.axis_index("wide")
    narrow_index = lax.axis_index("narrow")
    group_buckets = lax.dynamic_slice_in_dim(bucket, wide_index * members, members)
    group_lengths = lax.dynamic_slice_in_dim(dec_len, wide_index * members, members)
    ranks = rank_within(group_buckets)
    places = jnp.arange(members, dtype=jnp.int32)
    chosen = ranks == narrow_index
    source = jnp.sum(jnp.where(chosen, places, 0))
    length = jnp.sum(jnp.where(chosen, group_lengths, 0))
    own_slot = jnp.sum(jnp.where(places == narrow_index, ranks, 0))

    found = []
    enc_pieces, enc_offs = gather(
        grid, enc_weights, vector_hooks(grid, enc_vectors, dec_vectors, found)
    )
    enc_vec, dec_vec = gather_vectors(grid, enc_vectors, dec_vectors, found)
    enc_vec = enc_vec.astype(F32).reshape(-1, D)
    dec_vec = dec_vec.astype(F32).reshape(-1, D)
    first, second, third = encoder_parts(frames[0], enc_vec, enc_offs, enc_pieces)
    made = []

    def after_slot(values, ended):
        return barrier(tuple(values) + tuple(ended))[: len(values)]

    def hook_one(ended):
        made.append(first())
        return (made[-1][0],)

    def hook_two(ended):
        made.append(second(*after_slot(made[-1][:3], ended)))
        return (made[-1],)

    def hook_three(ended):
        o = after_slot((made[-1],), ended)[0]
        made.append(third(o, made[0][3]))
        return (made[-1],)

    hooks = [hook_one, hook_two, hook_three]
    dec_pieces, dec_offs = gather(grid, dec_weights, hooks)
    if not grid.fits:
        for hook in hooks:
            hook(())
    encoded = made[-1]
    if members == 2:
        other = grid.y_swap(encoded)
    else:
        every = lax.all_gather(encoded, "narrow", axis=0)
        other = lax.dynamic_index_in_dim(every, source, keepdims=False)
    flag = (source == narrow_index).astype(jnp.int32)[None]
    block_out, grad_inputs, grad_memory, saved, grad_rows = run_decoder(
        dec_in[0],
        cotangent[0],
        encoded,
        other,
        flag,
        length[None],
        dec_vec,
        dec_offs,
        dec_pieces,
        grid.core_swap if grid.fits else lambda value: value,
    )
    if members == 2:
        back = grid.y_swap(grad_memory.astype(BF16)).astype(F32)
    else:
        every = lax.all_gather(grad_memory.astype(BF16), "narrow", axis=0)
        back = lax.dynamic_index_in_dim(every, own_slot, keepdims=False).astype(F32)
    grad_encoded = jnp.where(own_slot == narrow_index, grad_memory, back)
    sums = [grad_rows]
    shard_stack = reduce_weights(grid, saved, sum_hooks(grid, sums))
    shard_vector = own_vectors(grid, sums[-1])
    return (block_out[None], grad_inputs[None], grad_encoded[None], shard_stack, shard_vector)


def solution(mesh):
    items = P(AXES, None, None)
    rows = P(AXES, None)
    line = P(AXES)
    return jax.shard_map(
        per_device,
        mesh=mesh,
        in_specs=(items, items, items, P(), P(), rows, line, rows, line),
        out_specs=(items, items, items, rows, line),
        check_vma=False,
    )
```
